32 devices in a mesh: tm: 8 (over z, y), mark: 4 (over x, core).
Axes of the slice: x: 2, y: 2, z: 4, core: 2. Of those that a mesh axis runs over, the one named last changes fastest.
Arguments:
- event_marks: int32 [32768], P('tm'), may hold values from 0 to 8191
- event_gaps: int32 [32768], P('tm'), may hold values from 1 to 65536, as said below
- excite: bfloat16 [512, 8192], P('mark'), may hold values from 0 to 0.59765625
- source: bfloat16 [512, 8192], P('mark'), may hold values from 0 to 0.59765625
- base_rate: float32 [8192], replicated, may hold values from 0.05 to 0.5
- weights: float32 [8], replicated, may hold values from 0.2 to 2
- decay_rates: float32 [8], replicated, may hold values from 1.0172526041666667e-06 to 0.06666667
Outputs:
- grad_excite: float32 [512, 8192], P('mark', 'tm')
- grad_source: float32 [512, 8192], P('mark', 'tm')
- grad_base: float32 [8192], P('tm')
The draws below stay inside these ranges and needn't reach their ends.
Inputs may be any that keep to these rules, and one draw needn't show every extreme that they name: `event_gaps`: ticks since the previous event, the first counted from time 0.
All inputs are finite; a program needn't handle non-finite values.
Results may differ from the reference program's by a relative error of at most 0.0003.
Values sent between devices are 32-bit elements; how exact they have to be, the bound alone decides.
A program may use at most 64 MiB of HBM per device.

```python
import math
import jax
import jax.numpy as jnp
from jax import lax

MARKS = 8192
RANK = 512
KERNEL_COUNT = 8
ARRIVAL_COUNT = 32768


def draw_event_gaps(key, part):
    first, latter_portion = jax.random.split(key)
    arrival_slot = jnp.arange(ARRIVAL_COUNT)
    upper_limit = 3 + 6 * arrival_slot // ARRIVAL_COUNT
    drawn_arrivals = jax.random.randint(first, (ARRIVAL_COUNT,), 1, upper_limit)
    cluster_moment = jax.random.randint(latter_portion, (3,), 0, ARRIVAL_COUNT)
    cluster_arrival_flags = jnp.any(arrival_slot[:, None] == cluster_moment[None, :], axis=1)
    return jnp.where(cluster_arrival_flags, 2 * ARRIVAL_COUNT, drawn_arrivals).astype(jnp.int32)


def draw_decay_rates(key, part):
    first, latter_portion = jax.random.split(key)
    ranking = jax.random.permutation(first, KERNEL_COUNT)
    kept_count = KERNEL_COUNT // 2
    slow_mask = ranking < kept_count
    spread = jax.random.uniform(latter_portion, (KERNEL_COUNT,), jnp.float32)
    slow_rate = jnp.exp(jnp.log(1.0 / (30.0 * ARRIVAL_COUNT)) + spread * jnp.log(6.0))
    fast_rate = jnp.exp(jnp.log(1.0 / 3000.0) + spread * jnp.log(200.0))
    return jnp.where(slow_mask, slow_rate, fast_rate).astype(jnp.float32)


def plant(entries, key, least, high):
    extent = entries.shape
    place = [jax.random.randint(jax.random.fold_in(key, axis), (), 0, extent[axis]) for axis in range(len(extent))]
    entries = entries.at[tuple(place)].set(least)
    longest = extent.index(max(extent))
    place[longest] = (place[longest] + 1) % extent[longest]
    return entries.at[tuple(place)].set(high)


def shard_levels(stream_key, shape, shards, low, top_value):
    def one(position, blocks):
        draws = jax.random.uniform(jax.random.fold_in(jax.random.fold_in(stream_key, 6), position), (blocks,), jnp.float32, low / len(shards), top_value / len(shards))
        return jnp.repeat(jnp.exp(draws), shape[position] // blocks).reshape((-1,) + (1,) * (len(shape) - position - 1))

    gain = one(*shards[0])
    for cut in shards[1:]:
        gain = gain * one(*cut)
    return gain


def setup_inputs(seed: int = 0) -> dict:
    splits = jax.random.split(jax.random.key(seed), 8)
    event_marks = plant(jax.random.randint(splits[0], (ARRIVAL_COUNT,), 0, MARKS), jax.random.fold_in(splits[0], 1), 0, MARKS - 1).astype(jnp.int32)
    event_gaps = draw_event_gaps(jax.random.fold_in(splits[7], 71), 0)
    excite = jnp.clip(0.59765625 * jax.random.uniform(splits[2], (RANK, MARKS), jnp.float32) ** shard_levels(splits[2], (RANK, MARKS), ((0, 4),), -0.2, 0.2), 0.0, 0.59765625).astype(jnp.bfloat16)
    source = jnp.clip(0.59765625 * jax.random.uniform(splits[3], (RANK, MARKS), jnp.float32) ** shard_levels(splits[3], (RANK, MARKS), ((0, 4),), -0.2, 0.2), 0.0, 0.59765625).astype(jnp.bfloat16)
    base_rate = jnp.clip(jnp.exp(jax.random.uniform(splits[4], (MARKS,), jnp.float32, math.log(0.05), math.log(0.5))), 0.05, 0.5)
    weights = jnp.clip(jnp.exp(jax.random.uniform(splits[5], (KERNEL_COUNT,), jnp.float32, math.log(0.2), math.log(2.0))), 0.2, 2.0)
    decay_rates = draw_decay_rates(jax.random.fold_in(splits[7], 71), 0)
    return {"event_marks": event_marks, "event_gaps": event_gaps, "excite": excite, "source": source, "base_rate": base_rate, "weights": weights, "decay_rates": decay_rates}


def decay_kernel(stamp_block, weights, decay_rates):
    block_size = stamp_block.shape[0]
    elapsed = jnp.maximum(stamp_block[:, None] - stamp_block[None, :], 0.0)
    causal = jnp.arange(block_size)[:, None] > jnp.arange(block_size)[None, :]
    accumulated = jnp.zeros((block_size, block_size), jnp.float32)
    for channel in range(decay_rates.shape[0]):
        accumulated = accumulated + weights[channel] * decay_rates[channel] * jnp.exp(-decay_rates[channel] * elapsed)
    return jnp.where(causal, accumulated, 0.0)


def reference(event_marks, event_gaps, excite, source, base_rate, weights, decay_rates):
    highest = lax.Precision.HIGHEST
    event_count = event_marks.shape[0]
    block_size = 512 if event_count % 512 == 0 else event_count
    block_count = event_count // block_size
    mark_count = excite.shape[1]
    dense_coupling = excite.shape[0]
    channels = decay_rates.shape[0]
    stamps = jnp.cumsum(event_gaps).astype(jnp.float32)
    t_end = stamps[-1]
    excite_full = excite.astype(jnp.float32).T
    source_complete = source.astype(jnp.float32).T
    excite_total = jnp.sum(excite_full, axis=0)
    anchors = jnp.concatenate([jnp.zeros((1,), jnp.float32), stamps[block_size - 1::block_size][:-1]])
    stamp_blocks = stamps.reshape(block_count, block_size)
    mark_blocks = event_marks.reshape(block_count, block_size)

    def forward(carry, pieces):
        carried, excite_sum, base_sum = carry
        stamp_block, mark_block, anchor = pieces
        values = source_complete[mark_block]
        factors = excite_full[mark_block]
        kernel = decay_kernel(stamp_block, weights, decay_rates)
        arrival = weights[None, :] * jnp.exp(-decay_rates[None, :] * (stamp_block - anchor)[:, None])
        excitation = jnp.dot(kernel, values, precision=highest) + jnp.dot(arrival, carried, precision=highest)
        intensity = base_rate[mark_block] + jnp.sum(factors * excitation, axis=1) / dense_coupling
        inverse = 1.0 / intensity
        end_time = stamp_block[-1]
        emission = decay_rates[:, None] * jnp.exp(-decay_rates[:, None] * (end_time - stamp_block)[None, :])
        carried = jnp.exp(-decay_rates * (end_time - anchor))[:, None] * carried + jnp.dot(emission, values, precision=highest)
        excite_sum = excite_sum.at[mark_block].add(inverse[:, None] * excitation)
        base_sum = base_sum.at[mark_block].add(inverse)
        return (carried, excite_sum, base_sum), inverse

    start = (jnp.zeros((channels, dense_coupling), jnp.float32), jnp.zeros((mark_count, dense_coupling), jnp.float32), jnp.zeros((mark_count,), jnp.float32))
    (carried, excite_sum, base_sum), inverses = lax.scan(forward, start, (stamp_blocks, mark_blocks, anchors))

    def backward(carry, pieces):
        pending, source_sum, integrated = carry
        stamp_block, mark_block, anchor, inverse = pieces
        values = source_complete[mark_block]
        weighted = inverse[:, None] * excite_full[mark_block]
        kernel = decay_kernel(stamp_block, weights, decay_rates)
        end_time = stamp_block[-1]
        reaching = weights[None, :] * jnp.exp(-decay_rates[None, :] * (end_time - stamp_block)[:, None])
        feedback = jnp.dot(kernel.T, weighted, precision=highest) + jnp.dot(reaching, pending, precision=highest)
        remainder = jnp.sum(weights[None, :] * (1.0 - jnp.exp(-decay_rates[None, :] * (t_end - stamp_block)[:, None])), axis=1)
        source_sum = source_sum.at[mark_block].add(feedback - remainder[:, None] * excite_total[None, :] / mark_count)
        integrated = integrated + jnp.dot(remainder, values, precision=highest)
        emission = decay_rates[:, None] * jnp.exp(-decay_rates[:, None] * (stamp_block - anchor)[None, :])
        pending = jnp.exp(-decay_rates * (end_time - anchor))[:, None] * pending + jnp.dot(emission, weighted, precision=highest)
        return (pending, source_sum, integrated), remainder

    start_back = (jnp.zeros((channels, dense_coupling), jnp.float32), jnp.zeros((mark_count, dense_coupling), jnp.float32), jnp.zeros((dense_coupling,), jnp.float32))
    (pending, source_sum, integrated), remainders = lax.scan(backward, start_back, (stamp_blocks, mark_blocks, anchors, inverses), reverse=True)
    factor = mark_count / event_count
    grad_excite = factor * excite_sum - integrated[None, :] / event_count
    grad_source = factor * source_sum
    grad_base = factor * base_sum - t_end / event_count
    return grad_excite.T, grad_source.T, grad_base
```

```python
import functools

import jax
import jax.numpy as jnp
from jax import lax
from jax.experimental import pallas as pl
from jax.experimental.pallas import tpu as pltpu
from jax.sharding import PartitionSpec as P

F32 = jnp.float32
BF16 = jnp.bfloat16
B = 128
HIGH = lax.Precision.HIGHEST
VMEM = pl.BlockSpec(memory_space=pltpu.VMEM)
SMEM = pl.BlockSpec(memory_space=pltpu.SMEM)
NT = (((1,), (1,)), ((), ()))


def iota(shape, axis):
    return lax.broadcasted_iota(jnp.int32, shape, axis)


def split(a):
    high = a.astype(BF16)
    return high, (a - high.astype(F32)).astype(BF16)


def dot(a, b):
    return jnp.dot(a, b, preferred_element_type=F32)


def two_term(a, b):
    high, low = split(a)
    n = a.shape[0]
    both = dot(jnp.concatenate([high.astype(F32), low.astype(F32)], 0).astype(BF16), b)
    return both[:n] + both[n:]


def down(ref, count, width=B):
    row = iota((count, width), 0)
    out = jnp.zeros((count, width), F32)
    for k in range(count):
        out = jnp.where(row == k, ref[k], out)
    return out


def across(ref, count, copies):
    lane = iota((1, B), 1)
    out = jnp.zeros((1, B), F32)
    for k in range(count):
        hit = (lane < copies * count) & (lax.rem(lane, count) == k)
        out = jnp.where(hit, ref[k], out)
    return out


def columns(u):
    blocks = u.shape[0]
    return jnp.concatenate([u, jnp.zeros((B - blocks, B), F32)], 0).T


def state_rows(state):
    high, low = split(state)
    high, low = high.astype(F32), low.astype(F32)
    fill = jnp.zeros((B - 3 * state.shape[0], state.shape[1]), F32)
    return jnp.concatenate([high, low, high, fill], 0).astype(BF16)


def state_lanes(a, count):
    high, low = split(a)
    lane = iota(a.shape, 1)
    return jnp.where(lane < 2 * count, high.astype(F32), low.astype(F32)).astype(BF16)


def gather_kernel(
    count, marks, decay, gaps, src, exc, srows, xrows, u_out, sums, device, xtot, tab_s, tab_x
):
    events, width = srows.shape
    blocks = events // B

    def turn(c, total):
        s = pl.ds(pl.multiple_of(c * B, B), B)
        tab_s[s, :] = src[:, s].astype(F32).T
        t = exc[:, s].astype(F32).T
        tab_x[s, :] = t
        return total + jnp.sum(t.reshape(B // 8, 8, width), axis=0)

    total = lax.fori_loop(0, src.shape[1] // B, turn, jnp.zeros((8, width), F32))
    xtot[...] = jnp.broadcast_to(jnp.sum(total, axis=0, keepdims=True), (8, width))

    def fetch(g, _):
        for j in range(16):
            e = g * 16 + j
            m = marks[e]
            srows[pl.ds(e, 1), :] = tab_s[pl.ds(m, 1), :]
            xrows[pl.ds(e, 1), :] = tab_x[pl.ds(m, 1), :]
        return 0

    lax.fori_loop(0, events // 16, fetch, 0)
    upper = (iota((B, B), 0) <= iota((B, B), 1)).astype(F32)
    u = jnp.dot(gaps[...].astype(F32), upper, precision=HIGH, preferred_element_type=F32)
    u_out[...] = u
    d, dw = down(decay, count), down(decay, count, width)
    state = jnp.zeros((count, width), F32)
    duration = jnp.zeros((1, 1), F32)
    for b in range(blocks):
        ub = u[b : b + 1, :]
        length = ub[:, B - 1 :]
        values = srows[b * B : (b + 1) * B, :].astype(BF16)
        part = two_term(d * jnp.exp(-d * (length - ub)), values)
        sums[b * count : (b + 1) * count, :] = part
        state = state * jnp.exp(-dw * length) + part
        duration = duration + length
    device[0:count, :] = state
    device[count:, :] = jnp.broadcast_to(duration, (8, width))


def inside_kernel(count, weights, decay, u_ref, marks, base, srows, sym, inside, lanes, base_e):
    blocks = u_ref.shape[0]
    u = u_ref[...]
    ut = columns(u)
    wide_d, wide_w = across(decay, count, 3), across(weights, count, 3)
    earlier = iota((B, B), 0) > iota((B, B), 1)
    bh, bl = split(base[...])
    base2 = jnp.concatenate([bh.astype(F32), bl.astype(F32)], 0).T.astype(BF16)
    groups = base.shape[0]
    for b in range(blocks):
        col = ut[:, b : b + 1]
        row = u[b : b + 1, :]
        apart = jnp.abs(col - row)
        g = jnp.zeros((B, B), F32)
        for k in range(count):
            g = g + (weights[k] * decay[k]) * jnp.exp(-decay[k] * apart)
        s = slice(b * B, (b + 1) * B)
        sym[s, :] = g
        high, low = split(jnp.where(earlier, g, 0.0))
        values = srows[s, :].astype(BF16)
        inside[s, :] = dot(high, values) + dot(low, values)
        lanes[s, :] = state_lanes(wide_w * jnp.exp(-wide_d * col), count)
        m = marks[b : b + 1, :]
        hi, lo = m // B, lax.rem(m, B)
        pick = (lax.rem(iota((2 * groups, B), 0), groups) == hi).astype(BF16)
        found = dot(base2, pick)
        base_e[b : b + 1, :] = jnp.sum(
            jnp.where(iota((B, B), 0) == lo, found, 0.0), axis=0, keepdims=True
        )


def forward_kernel(
    count, rank, weights, decay, place, u_ref, summaries, sums, lanes, inside, srows, xrows,
    excitation, partial, remain, misc,
):
    blocks = u_ref.shape[0]
    peers = summaries.shape[0]
    me = place[0]
    u = u_ref[...]
    width = srows.shape[1]
    d, w, dw = down(decay, count), down(weights, count), down(decay, count, width)
    state = jnp.zeros((count, width), F32)
    after = jnp.zeros((1, 1), F32)
    end = jnp.zeros((1, 1), F32)
    for r in range(peers):
        length = summaries[r, count : count + 1, 0:1]
        state = jnp.where(
            r < me, state * jnp.exp(-dw * length) + summaries[r, 0:count, :], state
        )
        after = after + jnp.where(r > me, length, 0.0)
        end = end + length
    ones = jnp.ones((8, width), BF16)
    for b in range(blocks):
        s = slice(b * B, (b + 1) * B)
        length = u[b : b + 1, B - 1 :]
        value = inside[s, :] + dot(lanes[s, :], state_rows(state))
        excitation[s, :] = value
        product = value * xrows[s, :]
        high, low = split(product)
        total = lax.dot_general(ones, high, NT, preferred_element_type=F32)
        total = total + lax.dot_general(ones, low, NT, preferred_element_type=F32)
        partial[b : b + 1, :] = total[0:1, :] * (1.0 / rank)
        state = state * jnp.exp(-dw * length) + sums[b * count : (b + 1) * count, :]
    comp = jnp.zeros((8, width), F32)
    for b in reversed(range(blocks)):
        s = slice(b * B, (b + 1) * B)
        ub = u[b : b + 1, :]
        length = ub[:, B - 1 :]
        left = jnp.sum(w * (1.0 - jnp.exp(-d * (length - ub + after))), axis=0, keepdims=True)
        remain[b : b + 1, :] = left
        comp = comp + two_term(jnp.broadcast_to(left, (8, B)), srows[s, :].astype(BF16))
        after = after + length
    misc[0:8, :] = comp
    misc[8:16, :] = jnp.broadcast_to(end, (8, width))


def reverse_kernel(count, decay, u_ref, marks, base_e, total, xrows, comp, inverse, sums, device, base_sum):
    blocks = u_ref.shape[0]
    u = u_ref[...]
    inv = 1.0 / (base_e[...] + total[...])
    inverse[...] = inv
    width = xrows.shape[1]
    d, dw = down(decay, count), down(decay, count, width)
    groups = base_sum.shape[0]
    pending = jnp.zeros((count, width), F32)
    both = jnp.zeros((2 * groups, B), F32)
    for b in reversed(range(blocks)):
        s = slice(b * B, (b + 1) * B)
        ub = u[b : b + 1, :]
        length = ub[:, B - 1 :]
        ib = inv[b : b + 1, :]
        part = two_term(d * jnp.exp(-d * ub) * ib, xrows[s, :].astype(BF16))
        sums[b * count : (b + 1) * count, :] = part
        pending = pending * jnp.exp(-dw * length) + part
        m = marks[b : b + 1, :]
        hi, lo = m // B, lax.rem(m, B)
        ih = ib.astype(BF16).astype(F32)
        spread = jnp.concatenate([jnp.broadcast_to(ih, (groups, B)), jnp.broadcast_to(ib - ih, (groups, B))], 0)
        left = jnp.where(lax.rem(iota((2 * groups, B), 0), groups) == hi, spread, 0.0).astype(BF16)
        right = (iota((B, B), 0) == lo).astype(BF16)
        both = both + lax.dot_general(left, right, NT, preferred_element_type=F32)
    base_sum[...] = both[:groups] + both[groups:]
    device[0:count, :] = pending
    device[count:, :] = comp[0:8, :]


def scatter(marks, values, out):
    def group(g, _):
        e = g * 4
        m = [marks[e + j] for j in range(4)]
        add = [values[pl.ds(e + j, 1), :] for j in range(4)]
        old = [out[pl.ds(r, 1), :] for r in m]
        for j in range(4):
            new = old[j] + add[j]
            for i in range(j):
                new = new + jnp.where(m[i] == m[j], add[i], 0.0)
            out[pl.ds(m[j], 1), :] = new
        return 0

    lax.fori_loop(0, values.shape[0] // 4, group, 0, unroll=4)


def clear(out):
    def zero(i, _):
        out[pl.ds(pl.multiple_of(i * 8, 8), 8), :] = jnp.zeros((8, out.shape[1]), F32)
        return 0

    lax.fori_loop(0, out.shape[0] // 8, zero, 0, unroll=8)


def scatter_excite_kernel(marks, inverse, excitation, out, values):
    blocks = inverse.shape[0]
    clear(out)
    cols = columns(inverse[...])
    for b in range(blocks):
        s = slice(b * B, (b + 1) * B)
        values[s, :] = excitation[s, :] * cols[:, b : b + 1]
    scatter(marks, values, out)


def scatter_source_kernel(
    count, weights, decay, place, marks, u_ref, inverse, remain, misc, xtot, summaries, back, sums, sym, xrows,
    out, fin, values,
):
    blocks = u_ref.shape[0]
    peers = summaries.shape[0]
    me = place[0]
    clear(out)
    u = u_ref[...]
    width = xrows.shape[1]
    dw = down(decay, count, width)
    wide_d, wide_w = across(decay, count, 3), across(weights, count, 3)
    pending = jnp.zeros((count, width), F32)
    comp = jnp.zeros((1, width), F32)
    for r in reversed(range(peers)):
        length = summaries[r, count : count + 1, 0:1]
        pending = jnp.where(r > me, pending * jnp.exp(-dw * length) + back[r, 0:count, :], pending)
        comp = comp + back[r, count : count + 1, :]
    fin[0:8, :] = jnp.broadcast_to(comp, (8, width))
    fin[8:16, :] = misc[8:16, :]
    ut, rem_t = columns(u), columns(remain[...])
    share = xtot[0:1, :] * (1.0 / out.shape[0])
    later = iota((B, B), 0) < iota((B, B), 1)
    for b in reversed(range(blocks)):
        s = slice(b * B, (b + 1) * B)
        length = u[b : b + 1, B - 1 :]
        high, low = split(jnp.where(later, sym[s, :] * inverse[b : b + 1, :], 0.0))
        x = xrows[s, :].astype(BF16)
        lanes = state_lanes(wide_w * jnp.exp(-wide_d * (length - ut[:, b : b + 1])), count)
        value = dot(high, x) + dot(low, x) + dot(lanes, state_rows(pending))
        values[s, :] = value - rem_t[:, b : b + 1] * share
        pending = pending * jnp.exp(-dw * length) + sums[b * count : (b + 1) * count, :]
    scatter(marks, values, out)


def call(kernel, ins, outs, scratch=(), flops=10**8):
    return pl.pallas_call(
        kernel,
        out_shape=[jax.ShapeDtypeStruct(s, t) for s, t in outs],
        in_specs=list(ins),
        out_specs=[VMEM] * len(outs),
        scratch_shapes=list(scratch),
        compiler_params=pltpu.CompilerParams(vmem_limit_bytes=40 * 2**20),
        cost_estimate=pl.CostEstimate(flops=flops, bytes_accessed=4 * 2**20, transcendentals=10**6),
    )


def body(marks, gaps, excite, source, base_rate, weights, decay):
    events = marks.shape[0]
    blocks = events // B
    slices, types = excite.shape
    rank = slices * lax.axis_size("mark")
    peers = lax.axis_size("tm")
    count = decay.shape[0]
    place = lax.axis_index("tm").reshape(1)
    flat = marks.reshape(blocks, B)
    rows = ((events, slices), F32)
    plane = ((blocks, B), F32)
    parts = ((blocks * count, slices), F32)
    packet = ((count + 8, slices), F32)

    srows, xrows, u, sums, device, xtot = call(
        functools.partial(gather_kernel, count),
        [SMEM, SMEM, VMEM, VMEM, VMEM],
        [rows, rows, plane, parts, packet, ((8, slices), F32)],
        [pltpu.VMEM((types, slices), F32)] * 2,
    )(marks, decay, gaps.reshape(blocks, B), source, excite)
    summaries = lax.all_gather(device, "tm")
    sym, inside, lanes, base_e = call(
        functools.partial(inside_kernel, count),
        [SMEM, SMEM] + [VMEM] * 4,
        [((events, B), F32), rows, ((events, B), BF16), plane],
        flops=5 * 10**9,
    )(weights, decay, u, flat, base_rate.reshape(types // B, B), srows)
    excitation, partial, remain, misc = call(
        functools.partial(forward_kernel, count, rank),
        [SMEM, SMEM, SMEM] + [VMEM] * 7,
        [rows, plane, plane, ((16, slices), F32)],
    )(weights, decay, place, u, summaries, sums, lanes, inside, srows, xrows)
    total = lax.psum(partial, "mark")
    inverse, back_sums, back_device, base_sum = call(
        functools.partial(reverse_kernel, count),
        [SMEM] + [VMEM] * 6,
        [plane, parts, packet, ((types // B, B), F32)],
    )(decay, u, flat, base_e, total, xrows, misc)
    back = lax.all_gather(back_device, "tm")
    (excite_term,) = call(
        scatter_excite_kernel,
        [SMEM] + [VMEM] * 2,
        [((types, slices), F32)],
        [pltpu.VMEM((events, slices), F32)],
        flops=10**10,
    )(marks, inverse, excitation)
    base_part = lax.psum_scatter(base_sum.reshape(types), "tm", scatter_dimension=0, tiled=True)
    excite_part = lax.psum_scatter(excite_term, "tm", scatter_dimension=0, tiled=True)
    source_term, fin = call(
        functools.partial(scatter_source_kernel, count),
        [SMEM] * 4 + [VMEM] * 10,
        [((types, slices), F32), ((16, slices), F32)],
        [pltpu.VMEM((events, slices), F32)],
        flops=10**10,
    )(weights, decay, place, marks, u, inverse, remain, misc, xtot, summaries, back, back_sums, sym, xrows)
    source_part = lax.psum_scatter(source_term, "tm", scatter_dimension=0, tiled=True)

    events_all = events * peers
    factor = types / events_all
    grad_excite = factor * excite_part.T - fin[0][:, None] / events_all
    grad_base = factor * base_part - fin[8, 0] / events_all
    return grad_excite, factor * source_part.T, grad_base


def solution(mesh):
    return jax.shard_map(
        body,
        mesh=mesh,
        in_specs=(P("tm"), P("tm"), P("mark", None), P("mark", None), P(), P(), P()),
        out_specs=(P("mark", "tm"), P("mark", "tm"), P("tm")),
        check_vma=False,
    )
```

```python
import functools

import jax
import jax.numpy as jnp
from jax import lax
from jax.experimental import pallas as pl
from jax.experimental.pallas import tpu as pltpu
from jax.sharding import PartitionSpec as P

F32 = jnp.float32
BF16 = jnp.bfloat16
B = 128
HIGH = lax.Precision.HIGHEST
VMEM = pl.BlockSpec(memory_space=pltpu.VMEM)
SMEM = pl.BlockSpec(memory_space=pltpu.SMEM)
NT = (((1,), (1,)), ((), ()))


def iota(shape, axis):
    return lax.broadcasted_iota(jnp.int32, shape, axis)


def split(a):
    high = a.astype(BF16)
    return high, (a - high.astype(F32)).astype(BF16)


def dot(a, b):
    return jnp.dot(a, b, preferred_element_type=F32)


def two_term(a, b):
    high, low = split(a)
    n = a.shape[0]
    both = dot(jnp.concatenate([high.astype(F32), low.astype(F32)], 0).astype(BF16), b)
    return both[:n] + both[n:]


def down(ref, count, width=B):
    row = iota((count, width), 0)
    out = jnp.zeros((count, width), F32)
    for k in range(count):
        out = jnp.where(row == k, ref[k], out)
    return out


def across(ref, count, copies):
    lane = iota((1, B), 1)
    out = jnp.zeros((1, B), F32)
    for k in range(count):
        hit = (lane < copies * count) & (lax.rem(lane, count) == k)
        out = jnp.where(hit, ref[k], out)
    return out


def columns(u):
    blocks = u.shape[0]
    return jnp.concatenate([u, jnp.zeros((B - blocks, B), F32)], 0).T


def state_rows(state):
    high, low = split(state)
    high, low = high.astype(F32), low.astype(F32)
    fill = jnp.zeros((B - 3 * state.shape[0], state.shape[1]), F32)
    return jnp.concatenate([high, low, high, fill], 0).astype(BF16)


def state_lanes(a, count):
    high, low = split(a)
    lane = iota(a.shape, 1)
    return jnp.where(lane < 2 * count, high.astype(F32), low.astype(F32)).astype(BF16)


def gather_kernel(
    count, marks, decay, gaps, src, exc, srows, xrows, u_out, sums, device, xtot, tab_s, tab_x
):
    events, width = srows.shape
    blocks = events // B

    def turn(c, total):
        s = pl.ds(pl.multiple_of(c * B, B), B)
        tab_s[s, :] = src[:, s].astype(F32).T
        t = exc[:, s].astype(F32).T
        tab_x[s, :] = t
        return total + jnp.sum(t.reshape(B // 8, 8, width), axis=0)

    total = lax.fori_loop(0, src.shape[1] // B, turn, jnp.zeros((8, width), F32))
    xtot[...] = jnp.broadcast_to(jnp.sum(total, axis=0, keepdims=True), (8, width))

    def fetch(g, _):
        for j in range(16):
            e = g * 16 + j
            m = marks[e]
            srows[pl.ds(e, 1), :] = tab_s[pl.ds(m, 1), :]
            xrows[pl.ds(e, 1), :] = tab_x[pl.ds(m, 1), :]
        return 0

    lax.fori_loop(0, events // 16, fetch, 0)
    upper = (iota((B, B), 0) <= iota((B, B), 1)).astype(F32)
    u = jnp.dot(gaps[...].astype(F32), upper, precision=HIGH, preferred_element_type=F32)
    u_out[...] = u
    d, dw = down(decay, count), down(decay, count, width)
    state = jnp.zeros((count, width), F32)
    duration = jnp.zeros((1, 1), F32)
    for b in range(blocks):
        ub = u[b : b + 1, :]
        length = ub[:, B - 1 :]
        values = srows[b * B : (b + 1) * B, :].astype(BF16)
        part = two_term(d * jnp.exp(-d * (length - ub)), values)
        sums[b * count : (b + 1) * count, :] = part
        state = state * jnp.exp(-dw * length) + part
        duration = duration + length
    device[0:count, :] = state
    device[count:, :] = jnp.broadcast_to(duration, (8, width))


def inside_kernel(count, weights, decay, u_ref, marks, base, srows, sym, inside, lanes, base_e):
    blocks = u_ref.shape[0]
    u = u_ref[...]
    ut = columns(u)
    wide_d, wide_w = across(decay, count, 3), across(weights, count, 3)
    earlier = iota((B, B), 0) > iota((B, B), 1)
    bh, bl = split(base[...])
    base2 = jnp.concatenate([bh.astype(F32), bl.astype(F32)], 0).T.astype(BF16)
    groups = base.shape[0]
    for b in range(blocks):
        col = ut[:, b : b + 1]
        row = u[b : b + 1, :]
        apart = jnp.abs(col - row)
        g = jnp.zeros((B, B), F32)
        for k in range(count):
            g = g + (weights[k] * decay[k]) * jnp.exp(-decay[k] * apart)
        s = slice(b * B, (b + 1) * B)
        sym[s, :] = g
        high, low = split(jnp.where(earlier, g, 0.0))
        values = srows[s, :].astype(BF16)
        inside[s, :] = dot(high, values) + dot(low, values)
        lanes[s, :] = state_lanes(wide_w * jnp.exp(-wide_d * col), count)
        m = marks[b : b + 1, :]
        hi, lo = m // B, lax.rem(m, B)
        pick = (lax.rem(iota((2 * groups, B), 0), groups) == hi).astype(BF16)
        found = dot(base2, pick)
        base_e[b : b + 1, :] = jnp.sum(
            jnp.where(iota((B, B), 0) == lo, found, 0.0), axis=0, keepdims=True
        )


def forward_kernel(
    count, rank, weights, decay, place, u_ref, summaries, sums, lanes, inside, srows, xrows,
    excitation, partial, remain, misc,
):
    blocks = u_ref.shape[0]
    peers = summaries.shape[0]
    me = place[0]
    u = u_ref[...]
    width = srows.shape[1]
    d, w, dw = down(decay, count), down(weights, count), down(decay, count, width)
    state = jnp.zeros((count, width), F32)
    after = jnp.zeros((1, 1), F32)
    end = jnp.zeros((1, 1), F32)
    for r in range(peers):
        length = summaries[r, count : count + 1, 0:1]
        state = jnp.where(
            r < me, state * jnp.exp(-dw * length) + summaries[r, 0:count, :], state
        )
        after = after + jnp.where(r > me, length, 0.0)
        end = end + length
    ones = jnp.ones((8, width), BF16)
    for b in range(blocks):
        s = slice(b * B, (b + 1) * B)
        length = u[b : b + 1, B - 1 :]
        value = inside[s, :] + dot(lanes[s, :], state_rows(state))
        excitation[s, :] = value
        product = value * xrows[s, :]
        high, low = split(product)
        total = lax.dot_general(ones, high, NT, preferred_element_type=F32)
        total = total + lax.dot_general(ones, low, NT, preferred_element_type=F32)
        partial[b : b + 1, :] = total[0:1, :] * (1.0 / rank)
        state = state * jnp.exp(-dw * length) + sums[b * count : (b + 1) * count, :]
    comp = jnp.zeros((8, width), F32)
    for b in reversed(range(blocks)):
        s = slice(b * B, (b + 1) * B)
        ub = u[b : b + 1, :]
        length = ub[:, B - 1 :]
        left = jnp.sum(w * (1.0 - jnp.exp(-d * (length - ub + after))), axis=0, keepdims=True)
        remain[b : b + 1, :] = left
        comp = comp + two_term(jnp.broadcast_to(left, (8, B)), srows[s, :].astype(BF16))
        after = after + length
    misc[0:8, :] = comp
    misc[8:16, :] = jnp.broadcast_to(end, (8, width))


def reverse_kernel(count, decay, u_ref, marks, base_e, total, xrows, comp, inverse, sums, device, base_sum):
    blocks = u_ref.shape[0]
    u = u_ref[...]
    inv = 1.0 / (base_e[...] + sum(total[r] for r in range(total.shape[0])))
    inverse[...] = inv
    width = xrows.shape[1]
    d, dw = down(decay, count), down(decay, count, width)
    groups = base_sum.shape[0]
    pending = jnp.zeros((count, width), F32)
    both = jnp.zeros((2 * groups, B), F32)
    for b in reversed(range(blocks)):
        s = slice(b * B, (b + 1) * B)
        ub = u[b : b + 1, :]
        length = ub[:, B - 1 :]
        ib = inv[b : b + 1, :]
        part = two_term(d * jnp.exp(-d * ub) * ib, xrows[s, :].astype(BF16))
        sums[b * count : (b + 1) * count, :] = part
        pending = pending * jnp.exp(-dw * length) + part
        m = marks[b : b + 1, :]
        hi, lo = m // B, lax.rem(m, B)
        ih = ib.astype(BF16).astype(F32)
        spread = jnp.concatenate([jnp.broadcast_to(ih, (groups, B)), jnp.broadcast_to(ib - ih, (groups, B))], 0)
        left = jnp.where(lax.rem(iota((2 * groups, B), 0), groups) == hi, spread, 0.0).astype(BF16)
        right = (iota((B, B), 0) == lo).astype(BF16)
        both = both + lax.dot_general(left, right, NT, preferred_element_type=F32)
    base_sum[...] = both[:groups] + both[groups:]
    device[0:count, :] = pending
    device[count:, :] = comp[0:8, :]


def scatter(marks, values, out):
    def group(g, _):
        e = g * 4
        m = [marks[e + j] for j in range(4)]
        add = [values[pl.ds(e + j, 1), :] for j in range(4)]
        old = [out[pl.ds(r, 1), :] for r in m]
        for j in range(4):
            new = old[j] + add[j]
            for i in range(j):
                new = new + jnp.where(m[i] == m[j], add[i], 0.0)
            out[pl.ds(m[j], 1), :] = new
        return 0

    lax.fori_loop(0, values.shape[0] // 4, group, 0, unroll=4)


def clear(out):
    def zero(i, _):
        out[pl.ds(pl.multiple_of(i * 8, 8), 8), :] = jnp.zeros((8, out.shape[1]), F32)
        return 0

    lax.fori_loop(0, out.shape[0] // 8, zero, 0, unroll=8)


def scatter_excite_kernel(marks, inverse, excitation, out, values):
    blocks = inverse.shape[0]
    clear(out)
    cols = columns(inverse[...])
    for b in range(blocks):
        s = slice(b * B, (b + 1) * B)
        values[s, :] = excitation[s, :] * cols[:, b : b + 1]
    scatter(marks, values, out)


def scatter_source_kernel(
    count, weights, decay, place, marks, u_ref, inverse, remain, misc, xtot, summaries, back, sums, sym, xrows,
    out, fin, values,
):
    blocks = u_ref.shape[0]
    peers = summaries.shape[0]
    me = place[0]
    clear(out)
    u = u_ref[...]
    width = xrows.shape[1]
    dw = down(decay, count, width)
    wide_d, wide_w = across(decay, count, 3), across(weights, count, 3)
    pending = jnp.zeros((count, width), F32)
    comp = jnp.zeros((1, width), F32)
    for r in reversed(range(peers)):
        length = summaries[r, count : count + 1, 0:1]
        pending = jnp.where(r > me, pending * jnp.exp(-dw * length) + back[r, 0:count, :], pending)
        comp = comp + back[r, count : count + 1, :]
    fin[0:8, :] = jnp.broadcast_to(comp, (8, width))
    fin[8:16, :] = misc[8:16, :]
    ut, rem_t = columns(u), columns(remain[...])
    share = xtot[0:1, :] * (1.0 / out.shape[0])
    later = iota((B, B), 0) < iota((B, B), 1)
    for b in reversed(range(blocks)):
        s = slice(b * B, (b + 1) * B)
        length = u[b : b + 1, B - 1 :]
        high, low = split(jnp.where(later, sym[s, :] * inverse[b : b + 1, :], 0.0))
        x = xrows[s, :].astype(BF16)
        lanes = state_lanes(wide_w * jnp.exp(-wide_d * (length - ut[:, b : b + 1])), count)
        value = dot(high, x) + dot(low, x) + dot(lanes, state_rows(pending))
        values[s, :] = value - rem_t[:, b : b + 1] * share
        pending = pending * jnp.exp(-dw * length) + sums[b * count : (b + 1) * count, :]
    scatter(marks, values, out)


def call(kernel, ins, outs, scratch=(), flops=10**8):
    return pl.pallas_call(
        kernel,
        out_shape=[jax.ShapeDtypeStruct(s, t) for s, t in outs],
        in_specs=list(ins),
        out_specs=[VMEM] * len(outs),
        scratch_shapes=list(scratch),
        compiler_params=pltpu.CompilerParams(vmem_limit_bytes=40 * 2**20),
        cost_estimate=pl.CostEstimate(flops=flops, bytes_accessed=4 * 2**20, transcendentals=10**6),
    )


def exchange_kernel(axis, n, spread, *refs):
    k = len(spread)
    ins, outs, send, recv = refs[:k], refs[k : 2 * k], refs[2 * k], refs[2 * k + 1]
    me = lax.axis_index(axis)
    peers = [lax.rem(me + i, n) for i in range(1, n)]
    barrier = pltpu.get_barrier_semaphore()
    for p in peers:
        pl.semaphore_signal(barrier, inc=1, device_id={axis: p}, device_id_type=pl.DeviceIdType.MESH)
    pl.semaphore_wait(barrier, n - 1)
    copies = []
    for a in range(k):
        for i, p in enumerate(peers):
            copy = pltpu.make_async_remote_copy(
                src_ref=ins[a].at[p] if spread[a] else ins[a],
                dst_ref=outs[a].at[me],
                send_sem=send.at[a, i],
                recv_sem=recv.at[a, i],
                device_id={axis: p},
                device_id_type=pl.DeviceIdType.MESH,
            )
            copy.start()
            copies.append(copy)
    for a in range(k):
        outs[a][me] = ins[a][me] if spread[a] else ins[a][...]
    for copy in copies:
        copy.wait()


def exchange(arrays, axis, spread, collective):
    n = lax.axis_size(axis)
    k = len(arrays)
    shapes = [a.shape if s else (n,) + a.shape for a, s in zip(arrays, spread)]
    return pl.pallas_call(
        functools.partial(exchange_kernel, axis, n, spread),
        out_shape=[jax.ShapeDtypeStruct(s, F32) for s in shapes],
        in_specs=[VMEM] * k,
        out_specs=[VMEM] * k,
        scratch_shapes=[pltpu.SemaphoreType.DMA((k, n - 1))] * 2,
        compiler_params=pltpu.CompilerParams(collective_id=collective, has_side_effects=True),
    )(*arrays)


def ring_kernel(n, x0, x1, out0, out1, slots, send, recv):
    xs, outs = (x0, x1), (out0, out1)
    per = out0.shape[0]
    half = per // 2
    me = lax.axis_index("tm")
    odd = lax.rem(me, 2)
    at = lax.div(me, 2) + odd * (lax.div(2 * n - 1 - me, 2) - lax.div(me, 2))

    def member(place):
        c = lax.rem(place + 2 * n, n)
        return 2 * c + lax.div(c, n // 2) * (2 * n - 1 - 4 * c)

    towards = (member(at + 1), member(at - 1))
    barrier = pltpu.get_barrier_semaphore()
    for p in towards:
        pl.semaphore_signal(barrier, inc=1, device_id={"tm": p}, device_id_type=pl.DeviceIdType.MESH)
    pl.semaphore_wait(barrier, 2)

    def rows(j, step):
        way = j % 2
        block = member(at + 1 + step) if way else member(at - 1 - step)
        return pl.ds(pl.multiple_of(block * per + way * half, 8), half)

    def copy(j, step, source):
        return pltpu.make_async_remote_copy(
            src_ref=source,
            dst_ref=slots.at[j, step],
            send_sem=send.at[j, step],
            recv_sem=recv.at[j, step],
            device_id={"tm": towards[j % 2]},
            device_id_type=pl.DeviceIdType.MESH,
        )

    for j in range(4):
        copy(j, 0, xs[j // 2].at[rows(j, 0)]).start()

    def step(s, _):
        for j in range(4):
            held = slots.at[j, s - 1]
            copy(j, s - 1, held).wait_recv()
            held[...] += xs[j // 2][rows(j, s), :]
            copy(j, s, held).start()
        return 0

    lax.fori_loop(1, n - 1, step, 0)
    for j in range(4):
        copy(j, n - 2, slots.at[j, n - 2]).wait_recv()
        start = (j % 2) * half
        own = pl.ds(pl.multiple_of(me * per + start, 8), half)
        outs[j // 2][start : start + half, :] = slots[j, n - 2] + xs[j // 2][own, :]

    def sent(s, _):
        for j in range(4):
            copy(j, s, slots.at[j, s]).wait_send()
        return 0

    lax.fori_loop(0, n - 1, sent, 0)


def ring_sum(x0, x1):
    n = lax.axis_size("tm")
    types, width = x0.shape
    per = types // n
    return pl.pallas_call(
        functools.partial(ring_kernel, n),
        out_shape=[jax.ShapeDtypeStruct((per, width), F32)] * 2,
        in_specs=[VMEM] * 2,
        out_specs=[VMEM] * 2,
        scratch_shapes=[
            pltpu.VMEM((4, n - 1, per // 2, width), F32),
            pltpu.SemaphoreType.DMA((4, n - 1)),
            pltpu.SemaphoreType.DMA((4, n - 1)),
        ],
        compiler_params=pltpu.CompilerParams(
            collective_id=3, has_side_effects=True, vmem_limit_bytes=40 * 2**20
        ),
    )(x0, x1)


def body(marks, gaps, excite, source, base_rate, weights, decay):
    events = marks.shape[0]
    blocks = events // B
    slices, types = excite.shape
    rank = slices * lax.axis_size("mark")
    peers = lax.axis_size("tm")
    count = decay.shape[0]
    place = lax.axis_index("tm").reshape(1)
    flat = marks.reshape(blocks, B)
    rows = ((events, slices), F32)
    plane = ((blocks, B), F32)
    parts = ((blocks * count, slices), F32)
    packet = ((count + 8, slices), F32)

    srows, xrows, u, sums, device, xtot = call(
        functools.partial(gather_kernel, count),
        [SMEM, SMEM, VMEM, VMEM, VMEM],
        [rows, rows, plane, parts, packet, ((8, slices), F32)],
        [pltpu.VMEM((types, slices), F32)] * 2,
    )(marks, decay, gaps.reshape(blocks, B), source, excite)
    (summaries,) = exchange([device], "tm", [False], 0)
    sym, inside, lanes, base_e = call(
        functools.partial(inside_kernel, count),
        [SMEM, SMEM] + [VMEM] * 4,
        [((events, B), F32), rows, ((events, B), BF16), plane],
        flops=5 * 10**9,
    )(weights, decay, u, flat, base_rate.reshape(types // B, B), srows)
    excitation, partial, remain, misc = call(
        functools.partial(forward_kernel, count, rank),
        [SMEM, SMEM, SMEM] + [VMEM] * 7,
        [rows, plane, plane, ((16, slices), F32)],
    )(weights, decay, place, u, summaries, sums, lanes, inside, srows, xrows)
    (total,) = exchange([partial], "mark", [False], 1)
    inverse, back_sums, back_device, base_sum = call(
        functools.partial(reverse_kernel, count),
        [SMEM] + [VMEM] * 6,
        [plane, parts, packet, ((types // B, B), F32)],
    )(decay, u, flat, base_e, total, xrows, misc)
    back, base_parts = exchange(
        [back_device, base_sum.reshape(peers, types // B // peers, B)], "tm", [False, True], 2
    )
    (excite_term,) = call(
        scatter_excite_kernel,
        [SMEM] + [VMEM] * 2,
        [((types, slices), F32)],
        [pltpu.VMEM((events, slices), F32)],
        flops=10**10,
    )(marks, inverse, excitation)
    source_term, fin = call(
        functools.partial(scatter_source_kernel, count),
        [SMEM] * 4 + [VMEM] * 10,
        [((types, slices), F32), ((16, slices), F32)],
        [pltpu.VMEM((events, slices), F32)],
        flops=10**10,
    )(weights, decay, place, marks, u, inverse, remain, misc, xtot, summaries, back, back_sums, sym, xrows)
    excite_part, source_part = ring_sum(excite_term, source_term)
    base_part = jnp.sum(base_parts, axis=0).reshape(types // peers)

    events_all = events * peers
    factor = types / events_all
    grad_excite = factor * excite_part.T - fin[0][:, None] / events_all
    grad_base = factor * base_part - fin[8, 0] / events_all
    return grad_excite, factor * source_part.T, grad_base


def solution(mesh):
    return jax.shard_map(
        body,
        mesh=mesh,
        in_specs=(P("tm"), P("tm"), P("mark", None), P("mark", None), P(), P(), P()),
        out_specs=(P("mark", "tm"), P("mark", "tm"), P("tm")),
        check_vma=False,
    )
```

```python
import functools

import jax
import jax.numpy as jnp
from jax import lax
from jax.experimental import pallas as pl
from jax.experimental.pallas import tpu as pltpu
from jax.sharding import PartitionSpec as P

F32 = jnp.float32
BF16 = jnp.bfloat16
B = 128
HIGH = lax.Precision.HIGHEST
VMEM = pl.BlockSpec(memory_space=pltpu.VMEM)
SMEM = pl.BlockSpec(memory_space=pltpu.SMEM)
NT = (((1,), (1,)), ((), ()))


def iota(shape, axis):
    return lax.broadcasted_iota(jnp.int32, shape, axis)


def split(a):
    high = a.astype(BF16)
    return high, (a - high.astype(F32)).astype(BF16)


def dot(a, b):
    return jnp.dot(a, b, preferred_element_type=F32)


def two_term(a, b):
    high, low = split(a)
    n = a.shape[0]
    both = dot(jnp.concatenate([high.astype(F32), low.astype(F32)], 0).astype(BF16), b)
    return both[:n] + both[n:]


def down(ref, count, width=B):
    row = iota((count, width), 0)
    out = jnp.zeros((count, width), F32)
    for k in range(count):
        out = jnp.where(row == k, ref[k], out)
    return out


def across(ref, count, copies):
    lane = iota((1, B), 1)
    out = jnp.zeros((1, B), F32)
    for k in range(count):
        hit = (lane < copies * count) & (lax.rem(lane, count) == k)
        out = jnp.where(hit, ref[k], out)
    return out


def columns(u):
    blocks = u.shape[0]
    return jnp.concatenate([u, jnp.zeros((B - blocks, B), F32)], 0).T


def state_rows(state):
    high, low = split(state)
    high, low = high.astype(F32), low.astype(F32)
    fill = jnp.zeros((B - 3 * state.shape[0], state.shape[1]), F32)
    return jnp.concatenate([high, low, high, fill], 0).astype(BF16)


def state_lanes(a, count):
    high, low = split(a)
    lane = iota(a.shape, 1)
    return jnp.where(lane < 2 * count, high.astype(F32), low.astype(F32)).astype(BF16)


def gather_kernel(
    count, marks, decay, gaps, src, exc, srows, xrows, u_out, sums, device, xtot, tab_s, tab_x
):
    events, width = srows.shape
    blocks = events // B

    def turn(c, total):
        s = pl.ds(pl.multiple_of(c * B, B), B)
        tab_s[s, :] = src[:, s].astype(F32).T
        t = exc[:, s].astype(F32).T
        tab_x[s, :] = t
        return total + jnp.sum(t.reshape(B // 8, 8, width), axis=0)

    total = lax.fori_loop(0, src.shape[1] // B, turn, jnp.zeros((8, width), F32))
    xtot[...] = jnp.broadcast_to(jnp.sum(total, axis=0, keepdims=True), (8, width))

    def fetch(g, _):
        for j in range(16):
            e = g * 16 + j
            m = marks[e]
            srows[pl.ds(e, 1), :] = tab_s[pl.ds(m, 1), :]
            xrows[pl.ds(e, 1), :] = tab_x[pl.ds(m, 1), :]
        return 0

    lax.fori_loop(0, events // 16, fetch, 0)
    upper = (iota((B, B), 0) <= iota((B, B), 1)).astype(F32)
    u = jnp.dot(gaps[...].astype(F32), upper, precision=HIGH, preferred_element_type=F32)
    u_out[...] = u
    d, dw = down(decay, count), down(decay, count, width)
    state = jnp.zeros((count, width), F32)
    duration = jnp.zeros((1, 1), F32)
    for b in range(blocks):
        ub = u[b : b + 1, :]
        length = ub[:, B - 1 :]
        values = srows[b * B : (b + 1) * B, :].astype(BF16)
        part = two_term(d * jnp.exp(-d * (length - ub)), values)
        sums[b * count : (b + 1) * count, :] = part
        state = state * jnp.exp(-dw * length) + part
        duration = duration + length
    device[0:count, :] = state
    device[count:, :] = jnp.broadcast_to(duration, (8, width))


def inside_kernel(count, weights, decay, u_ref, marks, base, srows, sym, inside, lanes, base_e):
    blocks = u_ref.shape[0]
    u = u_ref[...]
    ut = columns(u)
    wide_d, wide_w = across(decay, count, 3), across(weights, count, 3)
    earlier = iota((B, B), 0) > iota((B, B), 1)
    bh, bl = split(base[...])
    base2 = jnp.concatenate([bh.astype(F32), bl.astype(F32)], 0).T.astype(BF16)
    groups = base.shape[0]
    for b in range(blocks):
        col = ut[:, b : b + 1]
        row = u[b : b + 1, :]
        apart = jnp.abs(col - row)
        g = jnp.zeros((B, B), F32)
        for k in range(count):
            g = g + (weights[k] * decay[k]) * jnp.exp(-decay[k] * apart)
        s = slice(b * B, (b + 1) * B)
        sym[s, :] = g
        high, low = split(jnp.where(earlier, g, 0.0))
        values = srows[s, :].astype(BF16)
        inside[s, :] = dot(high, values) + dot(low, values)
        lanes[s, :] = state_lanes(wide_w * jnp.exp(-wide_d * col), count)
        m = marks[b : b + 1, :]
        hi, lo = m // B, lax.rem(m, B)
        pick = (lax.rem(iota((2 * groups, B), 0), groups) == hi).astype(BF16)
        found = dot(base2, pick)
        base_e[b : b + 1, :] = jnp.sum(
            jnp.where(iota((B, B), 0) == lo, found, 0.0), axis=0, keepdims=True
        )


def forward_kernel(
    count, rank, weights, decay, place, u_ref, summaries, sums, lanes, inside, srows, xrows,
    excitation, partial, remain, misc,
):
    blocks = u_ref.shape[0]
    peers = summaries.shape[0]
    me = place[0]
    u = u_ref[...]
    width = srows.shape[1]
    d, w, dw = down(decay, count), down(weights, count), down(decay, count, width)
    state = jnp.zeros((count, width), F32)
    after = jnp.zeros((1, 1), F32)
    end = jnp.zeros((1, 1), F32)
    for r in range(peers):
        length = summaries[r, count : count + 1, 0:1]
        state = jnp.where(
            r < me, state * jnp.exp(-dw * length) + summaries[r, 0:count, :], state
        )
        after = after + jnp.where(r > me, length, 0.0)
        end = end + length
    ones = jnp.ones((8, width), BF16)
    for b in range(blocks):
        s = slice(b * B, (b + 1) * B)
        length = u[b : b + 1, B - 1 :]
        value = inside[s, :] + dot(lanes[s, :], state_rows(state))
        excitation[s, :] = value
        product = value * xrows[s, :]
        high, low = split(product)
        total = lax.dot_general(ones, high, NT, preferred_element_type=F32)
        total = total + lax.dot_general(ones, low, NT, preferred_element_type=F32)
        partial[b : b + 1, :] = total[0:1, :] * (1.0 / rank)
        state = state * jnp.exp(-dw * length) + sums[b * count : (b + 1) * count, :]
    comp = jnp.zeros((8, width), F32)
    for b in reversed(range(blocks)):
        s = slice(b * B, (b + 1) * B)
        ub = u[b : b + 1, :]
        length = ub[:, B - 1 :]
        left = jnp.sum(w * (1.0 - jnp.exp(-d * (length - ub + after))), axis=0, keepdims=True)
        remain[b : b + 1, :] = left
        comp = comp + two_term(jnp.broadcast_to(left, (8, B)), srows[s, :].astype(BF16))
        after = after + length
    misc[0:8, :] = comp
    misc[8:16, :] = jnp.broadcast_to(end, (8, width))


def reverse_kernel(count, decay, u_ref, marks, base_e, total, xrows, comp, inverse, sums, device, base_sum):
    blocks = u_ref.shape[0]
    u = u_ref[...]
    inv = 1.0 / (base_e[...] + sum(total[r] for r in range(total.shape[0])))
    inverse[...] = inv
    width = xrows.shape[1]
    d, dw = down(decay, count), down(decay, count, width)
    groups = base_sum.shape[0]
    pending = jnp.zeros((count, width), F32)
    both = jnp.zeros((2 * groups, B), F32)
    for b in reversed(range(blocks)):
        s = slice(b * B, (b + 1) * B)
        ub = u[b : b + 1, :]
        length = ub[:, B - 1 :]
        ib = inv[b : b + 1, :]
        part = two_term(d * jnp.exp(-d * ub) * ib, xrows[s, :].astype(BF16))
        sums[b * count : (b + 1) * count, :] = part
        pending = pending * jnp.exp(-dw * length) + part
        m = marks[b : b + 1, :]
        hi, lo = m // B, lax.rem(m, B)
        ih = ib.astype(BF16).astype(F32)
        spread = jnp.concatenate([jnp.broadcast_to(ih, (groups, B)), jnp.broadcast_to(ib - ih, (groups, B))], 0)
        left = jnp.where(lax.rem(iota((2 * groups, B), 0), groups) == hi, spread, 0.0).astype(BF16)
        right = (iota((B, B), 0) == lo).astype(BF16)
        both = both + lax.dot_general(left, right, NT, preferred_element_type=F32)
    base_sum[...] = both[:groups] + both[groups:]
    device[0:count, :] = pending
    device[count:, :] = comp[0:8, :]


def scatter(marks, values, out):
    def group(g, _):
        e = g * 4
        m = [marks[e + j] for j in range(4)]
        add = [values[pl.ds(e + j, 1), :] for j in range(4)]
        old = [out[pl.ds(r, 1), :] for r in m]
        for j in range(4):
            new = old[j] + add[j]
            for i in range(j):
                new = new + jnp.where(m[i] == m[j], add[i], 0.0)
            out[pl.ds(m[j], 1), :] = new
        return 0

    lax.fori_loop(0, values.shape[0] // 4, group, 0, unroll=4)


def clear(out):
    def zero(i, _):
        out[pl.ds(pl.multiple_of(i * 8, 8), 8), :] = jnp.zeros((8, out.shape[1]), F32)
        return 0

    lax.fori_loop(0, out.shape[0] // 8, zero, 0, unroll=8)


def scatter_excite_kernel(marks, inverse, excitation, out, values):
    blocks = inverse.shape[0]
    clear(out)
    cols = columns(inverse[...])
    for b in range(blocks):
        s = slice(b * B, (b + 1) * B)
        values[s, :] = excitation[s, :] * cols[:, b : b + 1]
    scatter(marks, values, out)


def call(kernel, ins, outs, scratch=(), flops=10**8):
    return pl.pallas_call(
        kernel,
        out_shape=[jax.ShapeDtypeStruct(s, t) for s, t in outs],
        in_specs=list(ins),
        out_specs=[VMEM] * len(outs),
        scratch_shapes=list(scratch),
        compiler_params=pltpu.CompilerParams(vmem_limit_bytes=40 * 2**20),
        cost_estimate=pl.CostEstimate(flops=flops, bytes_accessed=4 * 2**20, transcendentals=10**6),
    )


def exchange_kernel(axis, n, spread, *refs):
    k = len(spread)
    ins, outs, send, recv = refs[:k], refs[k : 2 * k], refs[2 * k], refs[2 * k + 1]
    me = lax.axis_index(axis)
    peers = [lax.rem(me + i, n) for i in range(1, n)]
    barrier = pltpu.get_barrier_semaphore()
    for p in peers:
        pl.semaphore_signal(barrier, inc=1, device_id={axis: p}, device_id_type=pl.DeviceIdType.MESH)
    pl.semaphore_wait(barrier, n - 1)
    copies = []
    for a in range(k):
        for i, p in enumerate(peers):
            copy = pltpu.make_async_remote_copy(
                src_ref=ins[a].at[p] if spread[a] else ins[a],
                dst_ref=outs[a].at[me],
                send_sem=send.at[a, i],
                recv_sem=recv.at[a, i],
                device_id={axis: p},
                device_id_type=pl.DeviceIdType.MESH,
            )
            copy.start()
            copies.append(copy)
    for a in range(k):
        outs[a][me] = ins[a][me] if spread[a] else ins[a][...]
    for copy in copies:
        copy.wait()


def exchange(arrays, axis, spread, collective):
    n = lax.axis_size(axis)
    k = len(arrays)
    shapes = [a.shape if s else (n,) + a.shape for a, s in zip(arrays, spread)]
    return pl.pallas_call(
        functools.partial(exchange_kernel, axis, n, spread),
        out_shape=[jax.ShapeDtypeStruct(s, F32) for s in shapes],
        in_specs=[VMEM] * k,
        out_specs=[VMEM] * k,
        scratch_shapes=[pltpu.SemaphoreType.DMA((k, n - 1))] * 2,
        compiler_params=pltpu.CompilerParams(collective_id=collective, has_side_effects=True),
    )(*arrays)


def feedback_values(count, me, weights, decay, u_ref, inverse, remain, xtot, summaries, back, sums, sym, xrows, types, pair):
    blocks = u_ref.shape[0]
    peers = summaries.shape[0]
    u = u_ref[...]
    width = xrows.shape[1]
    dw = down(decay, count, width)
    wide_d, wide_w = across(decay, count, 3), across(weights, count, 3)
    pending = jnp.zeros((count, width), F32)
    for r in reversed(range(peers)):
        length = summaries[r, count : count + 1, 0:1]
        pending = jnp.where(r > me, pending * jnp.exp(-dw * length) + back[r, 0:count, :], pending)
    ut, rem_t = columns(u), columns(remain[...])
    share = xtot[0:1, :] * (1.0 / types)
    later = iota((B, B), 0) < iota((B, B), 1)
    for b in reversed(range(blocks)):
        s = slice(b * B, (b + 1) * B)
        length = u[b : b + 1, B - 1 :]
        high, low = split(jnp.where(later, sym[s, :] * inverse[b : b + 1, :], 0.0))
        x = xrows[s, :].astype(BF16)
        lanes = state_lanes(wide_w * jnp.exp(-wide_d * (length - ut[:, b : b + 1])), count)
        value = dot(high, x) + dot(low, x) + dot(lanes, state_rows(pending))
        value = value - rem_t[:, b : b + 1] * share
        high, low = split(value)
        pair[s, :] = jnp.concatenate([high.astype(F32), low.astype(F32)], 1).astype(BF16)
        pending = pending * jnp.exp(-dw * length) + sums[b * count : (b + 1) * count, :]


def ring_kernel(
    n, count, weights, decay, x0, marks, u_ref, inverse, remain, xtot, summaries, back, sums, sym, xrows,
    out0, out1, x1, pair, hot, slots, send, recv,
):
    xs, outs = (x0, x1), (out0, out1)
    per, width = out0.shape
    half = per // 2
    tile = hot.shape[0]
    me = lax.axis_index("tm")
    odd = lax.rem(me, 2)
    at = lax.div(me, 2) + odd * (lax.div(2 * n - 1 - me, 2) - lax.div(me, 2))

    def member(place):
        c = lax.rem(place + 2 * n, n)
        return 2 * c + lax.div(c, n // 2) * (2 * n - 1 - 4 * c)

    towards = (member(at + 1), member(at - 1))
    barrier = pltpu.get_barrier_semaphore()
    for p in towards:
        pl.semaphore_signal(barrier, inc=1, device_id={"tm": p}, device_id_type=pl.DeviceIdType.MESH)
    pl.semaphore_wait(barrier, 2)

    def rows(j, step):
        way = j % 2
        block = member(at + 1 + step) if way else member(at - 1 - step)
        return pl.ds(pl.multiple_of(block * per + way * half, 8), half)

    def copy(j, step, source):
        return pltpu.make_async_remote_copy(
            src_ref=source,
            dst_ref=slots.at[j, step],
            send_sem=send.at[j, step],
            recv_sem=recv.at[j, step],
            device_id={"tm": towards[j % 2]},
            device_id_type=pl.DeviceIdType.MESH,
        )

    def begin(chains):
        for j in chains:
            copy(j, 0, xs[j // 2].at[rows(j, 0)]).start()

    def step(s, chains):
        for j in chains:
            held = slots.at[j, s - 1]
            copy(j, s - 1, held).wait_recv()
            held[...] += xs[j // 2][rows(j, s), :]
            copy(j, s, held).start()

    def finish(chains):
        for j in chains:
            copy(j, n - 2, slots.at[j, n - 2]).wait_recv()
            start = (j % 2) * half
            own = pl.ds(pl.multiple_of(me * per + start, 8), half)
            outs[j // 2][start : start + half, :] = slots[j, n - 2] + xs[j // 2][own, :]

    def chunk(block):
        def part(t, _):
            first = block * per + t * tile
            kind = iota((tile, B), 0) + first
            for b in range(marks.shape[0]):
                hot[:, b * B : (b + 1) * B] = (kind == marks[b : b + 1, :]).astype(BF16)
            both = dot(hot[...], pair[...])
            x1[pl.ds(pl.multiple_of(first, 8), tile), :] = both[:, :width] + both[:, width:]
            return 0

        lax.fori_loop(0, per // tile, part, 0)

    begin((0, 1))
    feedback_values(
        count, me, weights, decay, u_ref, inverse, remain, xtot, summaries, back, sums, sym, xrows, x0.shape[0], pair
    )

    def excite_step(s, _):
        step(s, (0, 1))
        i = s - 1
        away = lax.div(i, 2) + 1
        chunk(member(at + away * (2 * lax.rem(i, 2) - 1)))
        return 0

    lax.fori_loop(1, n - 1, excite_step, 0)
    begin((2, 3))

    def rest(i, _):
        chunk(member(at + i * (n // 2)))
        return 0

    lax.fori_loop(0, 2, rest, 0)
    finish((0, 1))

    def source_step(s, _):
        step(s, (2, 3))
        return 0

    lax.fori_loop(1, n - 1, source_step, 0)
    finish((2, 3))

    def sent(s, _):
        for j in range(4):
            copy(j, s, slots.at[j, s]).wait_send()
        return 0

    lax.fori_loop(0, n - 1, sent, 0)


def ring_sum(count, weights, decay, x0, *rest):
    n = lax.axis_size("tm")
    types, width = x0.shape
    per = types // n
    events = rest[-1].shape[0]
    return pl.pallas_call(
        functools.partial(ring_kernel, n, count),
        out_shape=[jax.ShapeDtypeStruct((per, width), F32)] * 2,
        in_specs=[SMEM] * 2 + [VMEM] * (1 + len(rest)),
        out_specs=[VMEM] * 2,
        scratch_shapes=[
            pltpu.VMEM((types, width), F32),
            pltpu.VMEM((events, 2 * width), BF16),
            pltpu.VMEM((min(256, per), events), BF16),
            pltpu.VMEM((4, n - 1, per // 2, width), F32),
            pltpu.SemaphoreType.DMA((4, n - 1)),
            pltpu.SemaphoreType.DMA((4, n - 1)),
        ],
        compiler_params=pltpu.CompilerParams(
            collective_id=3, has_side_effects=True, vmem_limit_bytes=48 * 2**20
        ),
    )(weights, decay, x0, *rest)


def body(marks, gaps, excite, source, base_rate, weights, decay):
    events = marks.shape[0]
    blocks = events // B
    slices, types = excite.shape
    rank = slices * lax.axis_size("mark")
    peers = lax.axis_size("tm")
    count = decay.shape[0]
    place = lax.axis_index("tm").reshape(1)
    flat = marks.reshape(blocks, B)
    rows = ((events, slices), F32)
    plane = ((blocks, B), F32)
    parts = ((blocks * count, slices), F32)
    packet = ((count + 8, slices), F32)

    srows, xrows, u, sums, device, xtot = call(
        functools.partial(gather_kernel, count),
        [SMEM, SMEM, VMEM, VMEM, VMEM],
        [rows, rows, plane, parts, packet, ((8, slices), F32)],
        [pltpu.VMEM((types, slices), F32)] * 2,
    )(marks, decay, gaps.reshape(blocks, B), source, excite)
    (summaries,) = exchange([device], "tm", [False], 0)
    sym, inside, lanes, base_e = call(
        functools.partial(inside_kernel, count),
        [SMEM, SMEM] + [VMEM] * 4,
        [((events, B), F32), rows, ((events, B), BF16), plane],
        flops=5 * 10**9,
    )(weights, decay, u, flat, base_rate.reshape(types // B, B), srows)
    excitation, partial, remain, misc = call(
        functools.partial(forward_kernel, count, rank),
        [SMEM, SMEM, SMEM] + [VMEM] * 7,
        [rows, plane, plane, ((16, slices), F32)],
    )(weights, decay, place, u, summaries, sums, lanes, inside, srows, xrows)
    (total,) = exchange([partial], "mark", [False], 1)
    inverse, back_sums, back_device, base_sum = call(
        functools.partial(reverse_kernel, count),
        [SMEM] + [VMEM] * 6,
        [plane, parts, packet, ((types // B, B), F32)],
    )(decay, u, flat, base_e, total, xrows, misc)
    back, base_parts = exchange(
        [back_device, base_sum.reshape(peers, types // B // peers, B)], "tm", [False, True], 2
    )
    (excite_term,) = call(
        scatter_excite_kernel,
        [SMEM] + [VMEM] * 2,
        [((types, slices), F32)],
        [pltpu.VMEM((events, slices), F32)],
        flops=10**10,
    )(marks, inverse, excitation)
    excite_part, source_part = ring_sum(
        count, weights, decay, excite_term, flat, u, inverse, remain, xtot, summaries, back, back_sums, sym, xrows
    )
    comp = jnp.sum(back[:, count, :], axis=0)
    base_part = jnp.sum(base_parts, axis=0).reshape(types // peers)

    events_all = events * peers
    factor = types / events_all
    grad_excite = factor * excite_part.T - comp[:, None] / events_all
    grad_base = factor * base_part - misc[8, 0] / events_all
    return grad_excite, factor * source_part.T, grad_base


def solution(mesh):
    return jax.shard_map(
        body,
        mesh=mesh,
        in_specs=(P("tm"), P("tm"), P("mark", None), P("mark", None), P(), P(), P()),
        out_specs=(P("mark", "tm"), P("mark", "tm"), P("tm")),
        check_vma=False,
    )
```

```python
import functools

import jax
import jax.numpy as jnp
from jax import lax
from jax.experimental import pallas as pl
from jax.experimental.pallas import tpu as pltpu
from jax.sharding import PartitionSpec as P

F32 = jnp.float32
BF16 = jnp.bfloat16
B = 128
HIGH = lax.Precision.HIGHEST
VMEM = pl.BlockSpec(memory_space=pltpu.VMEM)
SMEM = pl.BlockSpec(memory_space=pltpu.SMEM)
NT = (((1,), (1,)), ((), ()))


def iota(shape, axis):
    return lax.broadcasted_iota(jnp.int32, shape, axis)


def split(a):
    high = a.astype(BF16)
    return high, (a - high.astype(F32)).astype(BF16)


def dot(a, b):
    return jnp.dot(a, b, preferred_element_type=F32)


def two_term(a, b):
    high, low = split(a)
    n = a.shape[0]
    both = dot(jnp.concatenate([high.astype(F32), low.astype(F32)], 0).astype(BF16), b)
    return both[:n] + both[n:]


def down(ref, count, width=B):
    row = iota((count, width), 0)
    out = jnp.zeros((count, width), F32)
    for k in range(count):
        out = jnp.where(row == k, ref[k], out)
    return out


def across(ref, count, copies):
    lane = iota((1, B), 1)
    out = jnp.zeros((1, B), F32)
    for k in range(count):
        hit = (lane < copies * count) & (lax.rem(lane, count) == k)
        out = jnp.where(hit, ref[k], out)
    return out


def columns(u):
    blocks = u.shape[0]
    return jnp.concatenate([u, jnp.zeros((B - blocks, B), F32)], 0).T


def state_rows(state):
    high, low = split(state)
    high, low = high.astype(F32), low.astype(F32)
    fill = jnp.zeros((B - 3 * state.shape[0], state.shape[1]), F32)
    return jnp.concatenate([high, low, high, fill], 0).astype(BF16)


def state_lanes(a, count):
    high, low = split(a)
    lane = iota(a.shape, 1)
    return jnp.where(lane < 2 * count, high.astype(F32), low.astype(F32)).astype(BF16)


def gather_kernel(
    count, marks, decay, gaps, src, exc, srows, xrows, u_out, sums, device, xtot, tab_s, tab_x
):
    events, width = srows.shape
    blocks = events // B

    def turn(c, total):
        s = pl.ds(pl.multiple_of(c * B, B), B)
        tab_s[s, :] = src[:, s].astype(F32).T
        t = exc[:, s].astype(F32).T
        tab_x[s, :] = t
        return total + jnp.sum(t.reshape(B // 8, 8, width), axis=0)

    total = lax.fori_loop(0, src.shape[1] // B, turn, jnp.zeros((8, width), F32))
    xtot[...] = jnp.broadcast_to(jnp.sum(total, axis=0, keepdims=True), (8, width))

    def fetch(g, _):
        for j in range(16):
            e = g * 16 + j
            m = marks[e]
            srows[pl.ds(e, 1), :] = tab_s[pl.ds(m, 1), :]
            xrows[pl.ds(e, 1), :] = tab_x[pl.ds(m, 1), :]
        return 0

    lax.fori_loop(0, events // 16, fetch, 0)
    upper = (iota((B, B), 0) <= iota((B, B), 1)).astype(F32)
    u = jnp.dot(gaps[...].astype(F32), upper, precision=HIGH, preferred_element_type=F32)
    u_out[...] = u
    d, dw = down(decay, count), down(decay, count, width)
    state = jnp.zeros((count, width), F32)
    duration = jnp.zeros((1, 1), F32)
    for b in range(blocks):
        ub = u[b : b + 1, :]
        length = ub[:, B - 1 :]
        values = srows[b * B : (b + 1) * B, :].astype(BF16)
        part = two_term(d * jnp.exp(-d * (length - ub)), values)
        sums[b * count : (b + 1) * count, :] = part
        state = state * jnp.exp(-dw * length) + part
        duration = duration + length
    device[0:count, :] = state
    device[count:, :] = jnp.broadcast_to(duration, (8, width))


def inside_kernel(count, weights, decay, u_ref, marks, base, srows, sym, inside, lanes, base_e):
    blocks = u_ref.shape[0]
    u = u_ref[...]
    ut = columns(u)
    wide_d, wide_w = across(decay, count, 3), across(weights, count, 3)
    earlier = iota((B, B), 0) > iota((B, B), 1)
    bh, bl = split(base[...])
    base2 = jnp.concatenate([bh.astype(F32), bl.astype(F32)], 0).T.astype(BF16)
    groups = base.shape[0]
    for b in range(blocks):
        col = ut[:, b : b + 1]
        row = u[b : b + 1, :]
        apart = jnp.abs(col - row)
        g = jnp.zeros((B, B), F32)
        for k in range(count):
            g = g + (weights[k] * decay[k]) * jnp.exp(-decay[k] * apart)
        s = slice(b * B, (b + 1) * B)
        sym[s, :] = g
        high, low = split(jnp.where(earlier, g, 0.0))
        values = srows[s, :].astype(BF16)
        inside[s, :] = dot(high, values) + dot(low, values)
        lanes[s, :] = state_lanes(wide_w * jnp.exp(-wide_d * col), count)
        m = marks[b : b + 1, :]
        hi, lo = m // B, lax.rem(m, B)
        pick = (lax.rem(iota((2 * groups, B), 0), groups) == hi).astype(BF16)
        found = dot(base2, pick)
        base_e[b : b + 1, :] = jnp.sum(
            jnp.where(iota((B, B), 0) == lo, found, 0.0), axis=0, keepdims=True
        )


def forward_kernel(
    count, rank, weights, decay, place, u_ref, summaries, sums, lanes, inside, srows, xrows,
    excitation, partial, remain, misc,
):
    blocks = u_ref.shape[0]
    peers = summaries.shape[0]
    me = place[0]
    u = u_ref[...]
    width = srows.shape[1]
    d, w, dw = down(decay, count), down(weights, count), down(decay, count, width)
    state = jnp.zeros((count, width), F32)
    after = jnp.zeros((1, 1), F32)
    end = jnp.zeros((1, 1), F32)
    for r in range(peers):
        length = summaries[r, count : count + 1, 0:1]
        state = jnp.where(
            r < me, state * jnp.exp(-dw * length) + summaries[r, 0:count, :], state
        )
        after = after + jnp.where(r > me, length, 0.0)
        end = end + length
    ones = jnp.ones((8, width), BF16)
    for b in range(blocks):
        s = slice(b * B, (b + 1) * B)
        length = u[b : b + 1, B - 1 :]
        value = inside[s, :] + dot(lanes[s, :], state_rows(state))
        excitation[s, :] = value
        product = value * xrows[s, :]
        high, low = split(product)
        total = lax.dot_general(ones, high, NT, preferred_element_type=F32)
        total = total + lax.dot_general(ones, low, NT, preferred_element_type=F32)
        partial[b : b + 1, :] = total[0:1, :] * (1.0 / rank)
        state = state * jnp.exp(-dw * length) + sums[b * count : (b + 1) * count, :]
    comp = jnp.zeros((8, width), F32)
    for b in reversed(range(blocks)):
        s = slice(b * B, (b + 1) * B)
        ub = u[b : b + 1, :]
        length = ub[:, B - 1 :]
        left = jnp.sum(w * (1.0 - jnp.exp(-d * (length - ub + after))), axis=0, keepdims=True)
        remain[b : b + 1, :] = left
        comp = comp + two_term(jnp.broadcast_to(left, (8, B)), srows[s, :].astype(BF16))
        after = after + length
    misc[0:8, :] = comp
    misc[8:16, :] = jnp.broadcast_to(end, (8, width))


def reverse_kernel(count, decay, u_ref, marks, base_e, total, xrows, comp, inverse, sums, device, base_sum):
    blocks = u_ref.shape[0]
    u = u_ref[...]
    inv = 1.0 / (base_e[...] + sum(total[r] for r in range(total.shape[0])))
    inverse[...] = inv
    width = xrows.shape[1]
    d, dw = down(decay, count), down(decay, count, width)
    groups = base_sum.shape[0]
    pending = jnp.zeros((count, width), F32)
    both = jnp.zeros((2 * groups, B), F32)
    for b in reversed(range(blocks)):
        s = slice(b * B, (b + 1) * B)
        ub = u[b : b + 1, :]
        length = ub[:, B - 1 :]
        ib = inv[b : b + 1, :]
        part = two_term(d * jnp.exp(-d * ub) * ib, xrows[s, :].astype(BF16))
        sums[b * count : (b + 1) * count, :] = part
        pending = pending * jnp.exp(-dw * length) + part
        m = marks[b : b + 1, :]
        hi, lo = m // B, lax.rem(m, B)
        ih = ib.astype(BF16).astype(F32)
        spread = jnp.concatenate([jnp.broadcast_to(ih, (groups, B)), jnp.broadcast_to(ib - ih, (groups, B))], 0)
        left = jnp.where(lax.rem(iota((2 * groups, B), 0), groups) == hi, spread, 0.0).astype(BF16)
        right = (iota((B, B), 0) == lo).astype(BF16)
        both = both + lax.dot_general(left, right, NT, preferred_element_type=F32)
    base_sum[...] = both[:groups] + both[groups:]
    device[0:count, :] = pending
    device[count:, :] = comp[0:8, :]


def scatter(marks, values, out):
    def group(g, _):
        e = g * 4
        m = [marks[e + j] for j in range(4)]
        add = [values[pl.ds(e + j, 1), :] for j in range(4)]
        old = [out[pl.ds(r, 1), :] for r in m]
        for j in range(4):
            new = old[j] + add[j]
            for i in range(j):
                new = new + jnp.where(m[i] == m[j], add[i], 0.0)
            out[pl.ds(m[j], 1), :] = new
        return 0

    lax.fori_loop(0, values.shape[0] // 4, group, 0, unroll=4)


def clear(out):
    def zero(i, _):
        out[pl.ds(pl.multiple_of(i * 8, 8), 8), :] = jnp.zeros((8, out.shape[1]), F32)
        return 0

    lax.fori_loop(0, out.shape[0] // 8, zero, 0, unroll=8)


def scatter_excite_kernel(marks, inverse, excitation, out, values):
    blocks = inverse.shape[0]
    clear(out)
    cols = columns(inverse[...])
    for b in range(blocks):
        s = slice(b * B, (b + 1) * B)
        values[s, :] = excitation[s, :] * cols[:, b : b + 1]
    scatter(marks, values, out)


def call(kernel, ins, outs, scratch=(), flops=10**8):
    return pl.pallas_call(
        kernel,
        out_shape=[jax.ShapeDtypeStruct(s, t) for s, t in outs],
        in_specs=list(ins),
        out_specs=[VMEM] * len(outs),
        scratch_shapes=list(scratch),
        compiler_params=pltpu.CompilerParams(vmem_limit_bytes=40 * 2**20),
        cost_estimate=pl.CostEstimate(flops=flops, bytes_accessed=4 * 2**20, transcendentals=10**6),
    )


def exchange_kernel(axis, n, spread, *refs):
    k = len(spread)
    ins, outs, send, recv = refs[:k], refs[k : 2 * k], refs[2 * k], refs[2 * k + 1]
    me = lax.axis_index(axis)
    peers = [lax.rem(me + i, n) for i in range(1, n)]
    barrier = pltpu.get_barrier_semaphore()
    for p in peers:
        pl.semaphore_signal(barrier, inc=1, device_id={axis: p}, device_id_type=pl.DeviceIdType.MESH)
    pl.semaphore_wait(barrier, n - 1)
    copies = []
    for a in range(k):
        for i, p in enumerate(peers):
            copy = pltpu.make_async_remote_copy(
                src_ref=ins[a].at[p] if spread[a] else ins[a],
                dst_ref=outs[a].at[me],
                send_sem=send.at[a, i],
                recv_sem=recv.at[a, i],
                device_id={axis: p},
                device_id_type=pl.DeviceIdType.MESH,
            )
            copy.start()
            copies.append(copy)
    for a in range(k):
        outs[a][me] = ins[a][me] if spread[a] else ins[a][...]
    for copy in copies:
        copy.wait()


def exchange(arrays, axis, spread, collective):
    n = lax.axis_size(axis)
    k = len(arrays)
    shapes = [a.shape if s else (n,) + a.shape for a, s in zip(arrays, spread)]
    return pl.pallas_call(
        functools.partial(exchange_kernel, axis, n, spread),
        out_shape=[jax.ShapeDtypeStruct(s, F32) for s in shapes],
        in_specs=[VMEM] * k,
        out_specs=[VMEM] * k,
        scratch_shapes=[pltpu.SemaphoreType.DMA((k, n - 1))] * 2,
        compiler_params=pltpu.CompilerParams(collective_id=collective, has_side_effects=True),
    )(*arrays)


def feedback_values(count, me, weights, decay, u_ref, inverse, remain, xtot, summaries, back, sums, sym, xrows, types, pair):
    blocks = u_ref.shape[0]
    peers = summaries.shape[0]
    u = u_ref[...]
    width = xrows.shape[1]
    dw = down(decay, count, width)
    wide_d, wide_w = across(decay, count, 3), across(weights, count, 3)
    pending = jnp.zeros((count, width), F32)
    for r in reversed(range(peers)):
        length = summaries[r, count : count + 1, 0:1]
        pending = jnp.where(r > me, pending * jnp.exp(-dw * length) + back[r, 0:count, :], pending)
    ut, rem_t = columns(u), columns(remain[...])
    share = xtot[0:1, :] * (1.0 / types)
    later = iota((B, B), 0) < iota((B, B), 1)
    for b in reversed(range(blocks)):
        s = slice(b * B, (b + 1) * B)
        length = u[b : b + 1, B - 1 :]
        high, low = split(jnp.where(later, sym[s, :] * inverse[b : b + 1, :], 0.0))
        x = xrows[s, :].astype(BF16)
        lanes = state_lanes(wide_w * jnp.exp(-wide_d * (length - ut[:, b : b + 1])), count)
        value = dot(high, x) + dot(low, x) + dot(lanes, state_rows(pending))
        value = value - rem_t[:, b : b + 1] * share
        high, low = split(value)
        pair[s, :] = jnp.concatenate([high.astype(F32), low.astype(F32)], 1).astype(BF16)
        pending = pending * jnp.exp(-dw * length) + sums[b * count : (b + 1) * count, :]


def ring_kernel(
    n, count, weights, decay, x0, marks, u_ref, inverse, remain, xtot, summaries, back, sums, sym, xrows,
    out0, out1, x1, pair, hot, slots, send, recv,
):
    xs, outs = (x0, x1), (out0, out1)
    per, width = out0.shape
    half = per // 2
    tile = hot.shape[0]
    me = lax.axis_index("tm")
    odd = lax.rem(me, 2)
    at = lax.div(me, 2) + odd * (lax.div(2 * n - 1 - me, 2) - lax.div(me, 2))

    def member(place):
        c = lax.rem(place + 2 * n, n)
        return 2 * c + lax.div(c, n // 2) * (2 * n - 1 - 4 * c)

    towards = (member(at + 1), member(at - 1))
    barrier = pltpu.get_barrier_semaphore()
    for p in towards:
        pl.semaphore_signal(barrier, inc=1, device_id={"tm": p}, device_id_type=pl.DeviceIdType.MESH)
    pl.semaphore_wait(barrier, 2)

    def rows(j, step):
        way = j % 2
        block = member(at + 1 + step) if way else member(at - 1 - step)
        return pl.ds(pl.multiple_of(block * per + way * half, 8), half)

    def copy(j, step, source):
        return pltpu.make_async_remote_copy(
            src_ref=source,
            dst_ref=slots.at[j, step],
            send_sem=send.at[j, step],
            recv_sem=recv.at[j, step],
            device_id={"tm": towards[j % 2]},
            device_id_type=pl.DeviceIdType.MESH,
        )

    def begin(chains):
        for j in chains:
            copy(j, 0, xs[j // 2].at[rows(j, 0)]).start()

    def step(s, chains):
        for j in chains:
            held = slots.at[j, s - 1]
            copy(j, s - 1, held).wait_recv()
            held[...] += xs[j // 2][rows(j, s), :]
            copy(j, s, held).start()

    def finish(chains):
        for j in chains:
            copy(j, n - 2, slots.at[j, n - 2]).wait_recv()
            start = (j % 2) * half
            own = pl.ds(pl.multiple_of(me * per + start, 8), half)
            outs[j // 2][start : start + half, :] = slots[j, n - 2] + xs[j // 2][own, :]

    def chunk(block):
        def part(t, _):
            first = block * per + t * tile
            kind = iota((tile, B), 0) + first
            for b in range(marks.shape[0]):
                hot[:, b * B : (b + 1) * B] = (kind == marks[b : b + 1, :]).astype(BF16)
            both = dot(hot[...], pair[...])
            x1[pl.ds(pl.multiple_of(first, 8), tile), :] = both[:, :width] + both[:, width:]
            return 0

        lax.fori_loop(0, per // tile, part, 0)

    begin((0, 1))
    feedback_values(
        count, me, weights, decay, u_ref, inverse, remain, xtot, summaries, back, sums, sym, xrows, x0.shape[0], pair
    )

    def excite_step(s, _):
        step(s, (0, 1))
        i = s - 1
        away = lax.div(i, 2) + 1
        chunk(member(at + away * (2 * lax.rem(i, 2) - 1)))
        return 0

    def two_steps(p, _):
        lax.fori_loop(2 * p + 1, 2 * p + 3, excite_step, 0)
        step(p, (2, 3))
        return 0

    lax.fori_loop(1, 3, excite_step, 0)
    begin((2, 3))
    lax.fori_loop(1, n // 2 - 1, two_steps, 0)

    def rest(i, _):
        chunk(member(at + i * (n // 2)))
        return 0

    lax.fori_loop(0, 2, rest, 0)
    finish((0, 1))

    def source_step(s, _):
        step(s, (2, 3))
        return 0

    lax.fori_loop(n // 2 - 1, n - 1, source_step, 0)
    finish((2, 3))

    def sent(s, _):
        for j in range(4):
            copy(j, s, slots.at[j, s]).wait_send()
        return 0

    lax.fori_loop(0, n - 1, sent, 0)


def ring_sum(count, weights, decay, x0, *rest):
    n = lax.axis_size("tm")
    types, width = x0.shape
    per = types // n
    events = rest[-1].shape[0]
    return pl.pallas_call(
        functools.partial(ring_kernel, n, count),
        out_shape=[jax.ShapeDtypeStruct((per, width), F32)] * 2,
        in_specs=[SMEM] * 2 + [VMEM] * (1 + len(rest)),
        out_specs=[VMEM] * 2,
        scratch_shapes=[
            pltpu.VMEM((types, width), F32),
            pltpu.VMEM((events, 2 * width), BF16),
            pltpu.VMEM((min(256, per), events), BF16),
            pltpu.VMEM((4, n - 1, per // 2, width), F32),
            pltpu.SemaphoreType.DMA((4, n - 1)),
            pltpu.SemaphoreType.DMA((4, n - 1)),
        ],
        compiler_params=pltpu.CompilerParams(
            collective_id=3, has_side_effects=True, vmem_limit_bytes=48 * 2**20
        ),
    )(weights, decay, x0, *rest)


def body(marks, gaps, excite, source, base_rate, weights, decay):
    events = marks.shape[0]
    blocks = events // B
    slices, types = excite.shape
    rank = slices * lax.axis_size("mark")
    peers = lax.axis_size("tm")
    count = decay.shape[0]
    place = lax.axis_index("tm").reshape(1)
    flat = marks.reshape(blocks, B)
    rows = ((events, slices), F32)
    plane = ((blocks, B), F32)
    parts = ((blocks * count, slices), F32)
    packet = ((count + 8, slices), F32)

    srows, xrows, u, sums, device, xtot = call(
        functools.partial(gather_kernel, count),
        [SMEM, SMEM, VMEM, VMEM, VMEM],
        [rows, rows, plane, parts, packet, ((8, slices), F32)],
        [pltpu.VMEM((types, slices), F32)] * 2,
    )(marks, decay, gaps.reshape(blocks, B), source, excite)
    (summaries,) = exchange([device], "tm", [False], 0)
    sym, inside, lanes, base_e = call(
        functools.partial(inside_kernel, count),
        [SMEM, SMEM] + [VMEM] * 4,
        [((events, B), F32), rows, ((events, B), BF16), plane],
        flops=5 * 10**9,
    )(weights, decay, u, flat, base_rate.reshape(types // B, B), srows)
    excitation, partial, remain, misc = call(
        functools.partial(forward_kernel, count, rank),
        [SMEM, SMEM, SMEM] + [VMEM] * 7,
        [rows, plane, plane, ((16, slices), F32)],
    )(weights, decay, place, u, summaries, sums, lanes, inside, srows, xrows)
    (total,) = exchange([partial], "mark", [False], 1)
    inverse, back_sums, back_device, base_sum = call(
        functools.partial(reverse_kernel, count),
        [SMEM] + [VMEM] * 6,
        [plane, parts, packet, ((types // B, B), F32)],
    )(decay, u, flat, base_e, total, xrows, misc)
    back, base_parts = exchange(
        [back_device, base_sum.reshape(peers, types // B // peers, B)], "tm", [False, True], 2
    )
    (excite_term,) = call(
        scatter_excite_kernel,
        [SMEM] + [VMEM] * 2,
        [((types, slices), F32)],
        [pltpu.VMEM((events, slices), F32)],
        flops=10**10,
    )(marks, inverse, excitation)
    excite_part, source_part = ring_sum(
        count, weights, decay, excite_term, flat, u, inverse, remain, xtot, summaries, back, back_sums, sym, xrows
    )
    comp = jnp.sum(back[:, count, :], axis=0)
    base_part = jnp.sum(base_parts, axis=0).reshape(types // peers)

    events_all = events * peers
    factor = types / events_all
    grad_excite = factor * excite_part.T - comp[:, None] / events_all
    grad_base = factor * base_part - misc[8, 0] / events_all
    return grad_excite, factor * source_part.T, grad_base


def solution(mesh):
    return jax.shard_map(
        body,
        mesh=mesh,
        in_specs=(P("tm"), P("tm"), P("mark", None), P("mark", None), P(), P(), P()),
        out_specs=(P("mark", "tm"), P("mark", "tm"), P("tm")),
        check_vma=False,
    )
```
